32 devices in a mesh: gx: 8 (over z, x), gy: 4 (over y, core).
Axes of the slice: x: 2, y: 2, z: 4, core: 2. Of those that a mesh axis runs over, the one named last changes fastest.
Arguments:
- field_in: bfloat16 [20, 32, 128, 1024], P(None, 'gx', 'gy'), may hold values from -6 to 6
- cotangent: bfloat16 [20, 32, 128, 1024], P(None, 'gx', 'gy'), may hold values from -6 to 6
- spec_weight: float32 [2, 192, 20, 20, 24, 24], P(None, 'gx', None, None, 'gy'), may hold values from -6 to 6
Outputs:
- grad_field: bfloat16 [20, 32, 128, 1024], P(None, 'gx', 'gy')
- grad_weight: float32 [2, 192, 20, 20, 24, 24], P(None, 'gx', None, None, 'gy')
The draws below stay inside these ranges and needn't reach their ends.
All inputs are finite; a program needn't handle non-finite values.
Results may differ from the reference program's by a relative error of at most 0.001.
Values sent between devices are 32-bit elements; how exact they have to be, the bound alone decides.
A program may use at most 512 MiB of HBM per device.

```python
import math
import jax
import jax.numpy as jnp
from jax import lax

C = 20
MX = 12
MY = 12
MZ = 12
MT = 8
Z = 64
T_SIZE = 16
X = 32
Y = 128
ZT = 1024
KX = 24
KY = 24
M = 192


def shard_levels(own_key, shape, split, smallest, top_value):
    def one(axis_at, parts):
        steps = jax.random.uniform(jax.random.fold_in(jax.random.fold_in(own_key, 6), axis_at), (parts,), jnp.float32, smallest / len(split), top_value / len(split))
        return jnp.repeat(jnp.exp(steps), shape[axis_at] // parts).reshape((-1,) + (1,) * (len(shape) - axis_at - 1))

    loudness = one(*split[0])
    for cut in split[1:]:
        loudness = loudness * one(*cut)
    return loudness


def centred(key, extent, spread, bound, shards=(), kind=jnp.bfloat16):
    loudness = shard_levels(key, extent, shards, -0.22, 0.18) if shards else 1.0
    result = jax.random.normal(key, extent, jnp.float32) * spread * loudness
    return jnp.minimum(jnp.maximum(result, -bound), bound).astype(kind)


def setup_inputs(seed: int = 0) -> dict:
    streams_of = jax.random.split(jax.random.key(seed), 4)
    return {
        "field_in": centred(streams_of[0], (C, X, Y, ZT), 1.0, 6.0, ((1, 8), (2, 4))),
        "cotangent": centred(streams_of[1], (C, X, Y, ZT), 1.0, 6.0, ((1, 8), (2, 4))),
        "spec_weight": centred(streams_of[2], (2, M, C, C, KX, KY), 1.0, 6.0, ((1, 8), (4, 4)), jnp.float32),
    }


def keep_modes(values, half_count, along_axis, length):
    lower_part = lax.slice_in_dim(values, 0, half_count, axis=along_axis)
    upper_part = lax.slice_in_dim(values, length - half_count, length, axis=along_axis)
    return jnp.concatenate([lower_part, upper_part], along_axis)

def place_modes(values, half_count, along_axis, length):
    lower_part = lax.slice_in_dim(values, 0, half_count, axis=along_axis)
    upper_part = lax.slice_in_dim(values, half_count, 2 * half_count, axis=along_axis)
    pad_shape = list(values.shape)
    pad_shape[along_axis] = length - 2 * half_count
    return jnp.concatenate([lower_part, jnp.zeros(pad_shape, values.dtype), upper_part], along_axis)

def spectrum(field):
    norm_factor = 1.0 / math.sqrt(X * Y * Z * T_SIZE)

    def channel_spectrum(plane):
        volume = plane.astype(jnp.float32).reshape(X, Y, Z, T_SIZE)
        coeffs = jnp.fft.rfftn(volume)
        coeffs = keep_modes(coeffs, MX, 0, X)
        coeffs = keep_modes(coeffs, MY, 1, Y)
        coeffs = keep_modes(coeffs, MZ, 2, Z)
        coeffs = coeffs[:, :, :, :MT].reshape(KX, KY, M) * norm_factor
        return jnp.stack([jnp.real(coeffs), jnp.imag(coeffs)])
    return jnp.transpose(lax.map(channel_spectrum, field), (1, 4, 0, 2, 3))

def reference(field_in, cotangent, spec_weight):
    forward_field = spectrum(field_in)
    forward_dual = spectrum(cotangent)
    doubling = jnp.where(jnp.arange(M) % MT == 0, 1.0, 2.0).astype(jnp.float32)
    widened = doubling[:, None, None, None]
    dual_real = forward_dual[0] * widened
    dual_imag = forward_dual[1] * widened
    field_real = forward_field[0]
    field_imag = forward_field[1]
    grad_real = field_real[:, :, None] * dual_real[:, None] + field_imag[:, :, None] * dual_imag[:, None]
    grad_imag = field_real[:, :, None] * dual_imag[:, None] - field_imag[:, :, None] * dual_real[:, None]
    grad_weight = jnp.stack([grad_real, grad_imag])
    back_real = lax.optimization_barrier(jnp.sum(spec_weight[0] * dual_real[:, None] + spec_weight[1] * dual_imag[:, None], axis=2))
    back_imag = lax.optimization_barrier(jnp.sum(spec_weight[0] * dual_imag[:, None] - spec_weight[1] * dual_real[:, None], axis=2))
    backward = jnp.transpose(jnp.stack([back_real, back_imag]), (2, 0, 3, 4, 1))
    norm_factor = math.sqrt(X * Y * Z * T_SIZE)

    def channel_field(paired):
        values = lax.complex(paired[0] / doubling, paired[1] / doubling).reshape(KX, KY, 2 * MZ, MT)
        values = place_modes(values, MX, 0, X)
        values = place_modes(values, MY, 1, Y)
        values = place_modes(values, MZ, 2, Z)
        pad_shape = (X, Y, Z, T_SIZE // 2 + 1 - MT)
        values = jnp.concatenate([values, jnp.zeros(pad_shape, values.dtype)], 3)
        volume = jnp.fft.irfftn(values, s=(X, Y, Z, T_SIZE)) * norm_factor
        return volume.reshape(X, Y, Z * T_SIZE)
    grad_field = lax.map(channel_field, backward)
    return (grad_field.astype(jnp.bfloat16), grad_weight)
```

```python
import functools
import math

import jax
import jax.numpy as jnp
import ml_dtypes
import numpy as np
from jax import lax
from jax.experimental import pallas as pl
from jax.experimental.pallas import tpu as pltpu
from jax.sharding import PartitionSpec as P

MX = 12
MY = 12
MZ = 12
MT = 8
Z = 64
T_SIZE = 16
KX = 24
KY = 24
M = 192
VMEM_LIMIT = 56 * 1024 * 1024

minor_contract = (((1,), (1,)), ((), ()))
plain_contract = (((1,), (0,)), ((), ()))
lead_contract = (((0,), (0,)), ((), ()))


def signed(count, half):
    ladder = np.arange(count)
    return np.where(ladder < half, ladder, ladder - 2 * half)


def split(table):
    table = np.asarray(table, np.float32)
    high = table.astype(ml_dtypes.bfloat16)
    low = (table - high.astype(np.float32)).astype(ml_dtypes.bfloat16)
    return high, low


def pair_table(count, half, length):
    residue = (signed(count, half)[:, None] * np.arange(length)[None, :]) % length
    phases = residue * (2.0 * math.pi / length)
    cosine = np.cos(phases) / math.sqrt(length)
    sine = np.sin(phases) / math.sqrt(length)
    return np.stack([np.stack([cosine, sine]), np.stack([-sine, cosine])])


def depth_table():
    cells = np.arange(Z * T_SIZE)
    modes = np.arange(M)
    depth_freq = signed(2 * MZ, MZ)[modes // MT]
    residue = (
        depth_freq[:, None] * (cells // T_SIZE)[None, :] * T_SIZE
        + (modes % MT)[:, None] * (cells % T_SIZE)[None, :] * Z
    ) % (Z * T_SIZE)
    phases = residue * (2.0 * math.pi / (Z * T_SIZE))
    scale = 1.0 / math.sqrt(Z * T_SIZE)
    return np.concatenate([np.cos(phases) * scale, -np.sin(phases) * scale])


def y_blocks(y_count, y_groups, x_local):
    table = pair_table(KY, MY, y_count).reshape(2, 2, KY, y_groups, -1)
    full = np.einsum("pqkgy,xw->gqxypwk", table, np.eye(x_local))
    return full.reshape(y_groups, 2 * x_local * table.shape[-1], 2 * x_local * KY)


def x_blocks(x_count, x_groups):
    table = pair_table(KX, MX, x_count).reshape(2, 2, KX, x_groups, -1)
    full = np.einsum("pqksx,yw->sqxykpw", table, np.eye(KY))
    return full.reshape(x_groups, 2 * table.shape[-1] * KY, KX * 2 * KY)


def halves(values):
    high = values.astype(jnp.bfloat16)
    return high, (values - high.astype(jnp.float32)).astype(jnp.bfloat16)


def mul(a, b, contract):
    return lax.dot_general(a, b, contract, preferred_element_type=jnp.float32)


def product(values, high, low, contract):
    v_high, v_low = halves(values)
    return (
        mul(v_high, low, contract) + mul(v_low, high, contract) + mul(v_high, high, contract)
    )


def params():
    return pltpu.CompilerParams(vmem_limit_bytes=VMEM_LIMIT)


def whole(shape):
    return pl.BlockSpec(shape, lambda *_: (0,) * len(shape))


def zt_y_kernel(rows_m, order, f_ref, g_ref, table, wh, wl, out):
    cells = jnp.concatenate(
        [ref[0].reshape(-1, ref.shape[-1]) for ref in (f_ref, g_ref)], axis=0
    )
    doubled = mul(table[...], cells, minor_contract)
    spectrum = doubled[: 2 * M] + doubled[2 * M :]
    half = spectrum.shape[1] // 2
    both = jnp.concatenate(
        [
            jnp.concatenate([spectrum[:M, at : at + half], spectrum[M:, at : at + half]], axis=1)
            for at in (0, half)
        ],
        axis=0,
    )
    planes = product(both, wh[0], wl[0], plain_contract)
    joined = jnp.concatenate([planes[:M], planes[M:]], axis=1)
    if rows_m % 8 == 0:
        out[0, :, 0] = joined.reshape(-1, rows_m, joined.shape[-1])
    else:
        out[0, 0] = joined


def x_kernel(last, r_ref, wh, wl, out, acc):
    step = pl.program_id(0)
    width = wh.shape[1]
    share = out.shape[2] // 2

    @pl.when(step == 0)
    def _():
        acc[...] = jnp.zeros_like(acc)

    for field in range(2):
        acc[field] += product(
            r_ref[0, :, field * width : (field + 1) * width], wh[0], wl[0], plain_contract
        )

    @pl.when(step == last)
    def _():
        for g in range(out.shape[0]):
            for field in range(2):
                out[g, :, field * share : (field + 1) * share] = acc[
                    field, :, g * share : (g + 1) * share
                ]


def back_kernel(v_ref, w_ref, s_ref, out, left, dual):
    share = v_ref.shape[2] // 2
    channels, kx_local = s_ref.shape[2:4]

    @pl.when(pl.program_id(0) == 0)
    def _():
        def one(o, carry):
            row = v_ref[o] * w_ref[...]
            row = jnp.concatenate([row, jnp.zeros((row.shape[0], 128), jnp.float32)], axis=1)
            for k in range(kx_local):
                at = 2 * k * KY
                real, imag = row[:, at : at + 128], row[:, at + KY : at + KY + 128]
                left[0, 0, o, k] = real
                left[0, 1, o, k] = -imag
                left[1, 0, o, k] = imag
                left[1, 1, o, k] = real
                at += share
                dual[0, o, k] = row[:, at : at + 128]
                dual[1, o, k] = row[:, at + KY : at + KY + 128]
            return carry

        lax.fori_loop(0, v_ref.shape[0], one, 0)

    for k in range(kx_local):
        real = jnp.zeros(s_ref.shape[4:], jnp.float32)
        imag = jnp.zeros(s_ref.shape[4:], jnp.float32)
        for o in range(channels):
            d_real, d_imag = dual[0, o, k, :, :KY], dual[1, o, k, :, :KY]
            s_real, s_imag = s_ref[0, 0, o, k], s_ref[1, 0, o, k]
            real += s_real * d_real + s_imag * d_imag
            imag += s_real * d_imag - s_imag * d_real
        at = 2 * k * KY
        out[0, :, at : at + KY] = real
        out[0, :, at + KY : at + 2 * KY] = imag


def x_back_kernel(b_ref, wh, wl, out, held):
    share = b_ref.shape[2]

    @pl.when(pl.program_id(0) == 0)
    def _():
        for g in range(b_ref.shape[0]):
            held[:, g * share : (g + 1) * share] = b_ref[g]

    out[0] = product(held[...], wh[0], wl[0], minor_contract)


def y_zt_back_kernel(order, q_ref, th, tl, wh, wl, *rest):
    out = rest[-1]
    rows = q_ref[...].reshape(M, q_ref.shape[-1])
    planes = product(rows, wh[0], wl[0], minor_contract)
    half = planes.shape[1] // 2
    stacked = jnp.concatenate([planes[:, :half], planes[:, half:]], axis=0)
    cells = product(stacked, th[...], tl[...], lead_contract)
    out[0] = cells.reshape(out.shape[1:]).astype(out.dtype)


def per_device(field_in, cotangent, spec_weight):
    channels, x_local, y_local, depth_time = field_in.shape
    n = lax.axis_size("gx")
    groups = lax.axis_size("gy")
    x_count, y_count = x_local * n, y_local * groups
    m_local = M // n
    kx_local = KX // groups
    c_local = channels // groups
    width = 2 * x_local * KY
    share = kx_local * 2 * KY
    cells = x_local * y_local
    aligned = m_local % 8 == 0
    me = lax.axis_index("gy")

    t_high, t_low = split(depth_table())
    t_both = np.concatenate([t_high, t_low])
    y_high, y_low = split(y_blocks(y_count, groups, x_local))
    x_high, x_low = split(x_blocks(x_count, n))

    ladder = lax.iota(jnp.int32, 2 * c_local)

    def order_of(first, second):
        owners = jnp.where(ladder < c_local, first, second)
        ids = owners * c_local + ladder % c_local
        return jnp.concatenate([ids, me[None]]).astype(jnp.int32)

    near = order_of(me, me ^ 2)
    far = order_of(me ^ 1, me ^ 3)
    count = 2 * c_local

    def field_spec():
        return pl.BlockSpec((1, x_local, y_local, depth_time), lambda i, o: (o[i], 0, 0, 0))

    def y_spec():
        return pl.BlockSpec((1, 2 * cells, width), lambda i, o: (o[count], 0, 0))

    if aligned:
        block = pl.BlockSpec(
            (1, n, 1, m_local, 2 * width), lambda i, o: (i // c_local, 0, i % c_local, 0, 0)
        )
        shape = (2, n, c_local, m_local, 2 * width)
    else:
        block = pl.BlockSpec(
            (1, 1, M, 2 * width), lambda i, o: (i // c_local, i % c_local, 0, 0)
        )
        shape = (2, c_local, M, 2 * width)

    def forward(order):
        result = pl.pallas_call(
            functools.partial(zt_y_kernel, m_local),
            out_shape=jax.ShapeDtypeStruct(shape, jnp.float32),
            grid_spec=pltpu.PrefetchScalarGridSpec(
                num_scalar_prefetch=1,
                grid=(count,),
                in_specs=[field_spec(), field_spec()]
                + [whole((4 * M, depth_time))]
                + [y_spec(), y_spec()],
                out_specs=block,
            ),
            compiler_params=params(),
            cost_estimate=pl.CostEstimate(
                flops=count * 2 * (4 * 2 * M * depth_time * cells + 6 * M * 2 * cells * width),
                bytes_accessed=count * (4 * cells * depth_time + 8 * M * width),
                transcendentals=0,
            ),
        )(order, field_in, cotangent, t_both, y_high, y_low)
        if not aligned:
            result = result.reshape(2, c_local, n, m_local, 2 * width).transpose(0, 2, 1, 3, 4)
        return result

    swap_core = [(d, d ^ 1) for d in range(groups)]
    swap_y = [(d, d ^ 2) for d in range(groups)]

    away = forward(far)
    arrived = lax.ppermute(away, "gy", swap_core)
    kept = forward(near)
    passed = lax.ppermute(kept[1] + arrived[1], "gy", swap_y)
    summed = (kept[0] + arrived[0]) + passed

    section = lax.all_to_all(summed, "gx", split_axis=0, concat_axis=0, tiled=True)
    rows = c_local * m_local
    section = section.reshape(n, rows, 2 * width)
    x_spec = pl.BlockSpec((1, width, groups * share), lambda s: (s, 0, 0))
    at_kx = pl.pallas_call(
        functools.partial(x_kernel, n - 1),
        out_shape=jax.ShapeDtypeStruct((groups, rows, 2 * share), jnp.float32),
        grid=(n,),
        in_specs=[pl.BlockSpec((1, rows, 2 * width), lambda s: (s, 0, 0)), x_spec, x_spec],
        out_specs=whole((groups, rows, 2 * share)),
        scratch_shapes=[pltpu.VMEM((2, rows, groups * share), jnp.float32)],
        compiler_params=params(),
    )(section, x_high, x_low)
    modes = lax.all_to_all(at_kx, "gy", split_axis=0, concat_axis=0, tiled=True)
    modes = modes.reshape(channels, m_local, 2 * share)

    mode_ids = lax.axis_index("gx") * m_local + lax.iota(jnp.int32, m_local)
    doubling = jnp.where(mode_ids % MT == 0, 1.0, 2.0).astype(jnp.float32)
    lanes = lax.iota(jnp.int32, 2 * share)[None]
    doubling = jnp.where(lanes < share, 1.0, doubling[:, None])

    weights = jnp.transpose(spec_weight, (0, 2, 3, 4, 1, 5))
    unpacked = (channels, kx_local, m_local, 128)
    padded = 2 * channels * channels * kx_local * m_local * 128 * 4
    backward, left, dual = pl.pallas_call(
        back_kernel,
        out_shape=[
            jax.ShapeDtypeStruct((channels, m_local, share), jnp.float32),
            jax.ShapeDtypeStruct((2, 2) + unpacked, jnp.float32),
            jax.ShapeDtypeStruct((2,) + unpacked, jnp.float32),
        ],
        grid=(channels,),
        in_specs=[
            whole((channels, m_local, 2 * share)),
            whole((m_local, 2 * share)),
            pl.BlockSpec((2, 1, channels, kx_local, m_local, KY), lambda i: (0, i, 0, 0, 0, 0)),
        ],
        out_specs=[
            pl.BlockSpec((1, m_local, share), lambda i: (i, 0, 0)),
            whole((2, 2) + unpacked),
            whole((2,) + unpacked),
        ],
        compiler_params=params(),
        cost_estimate=pl.CostEstimate(flops=2 * padded, bytes_accessed=padded, transcendentals=0),
    )(modes, doubling, weights)

    spread = lax.all_to_all(
        backward.reshape(groups, rows, share), "gy", split_axis=0, concat_axis=0, tiled=True
    )
    left, dual = left[..., None, :, :, :KY], dual[:, None, None, ..., :KY]
    grad_weight = left[0] * dual[0] + left[1] * dual[1]
    grad_weight = jnp.transpose(grad_weight, (0, 4, 1, 2, 3, 5))

    planes = pl.pallas_call(
        x_back_kernel,
        out_shape=jax.ShapeDtypeStruct((n, rows, width), jnp.float32),
        grid=(n,),
        in_specs=[whole((groups, rows, share)), x_spec, x_spec],
        out_specs=pl.BlockSpec((1, rows, width), lambda s: (s, 0, 0)),
        scratch_shapes=[pltpu.VMEM((rows, groups * share), jnp.float32)],
        compiler_params=params(),
    )(spread, x_high, x_low)
    own = lax.all_to_all(planes, "gx", split_axis=0, concat_axis=0, tiled=True)
    own = own.reshape(n, c_local, m_local, width)
    crossed = lax.ppermute(own, "gy", swap_y)
    crossed, grad_weight = lax.optimization_barrier((crossed, grad_weight))
    pair = jnp.stack([own, crossed])
    other = lax.ppermute(pair, "gy", swap_core)

    def inverse(order, values, target):
        if aligned:
            spec = pl.BlockSpec(
                (1, n, 1, m_local, width), lambda i, o: (i // c_local, 0, i % c_local, 0, 0)
            )
        else:
            values = values.transpose(0, 2, 1, 3, 4).reshape(2, c_local, M, width)
            spec = pl.BlockSpec(
                (1, 1, M, width), lambda i, o: (i // c_local, i % c_local, 0, 0)
            )
        extra = [] if target is None else [target]
        return pl.pallas_call(
            y_zt_back_kernel,
            out_shape=jax.ShapeDtypeStruct(field_in.shape, jnp.bfloat16),
            grid_spec=pltpu.PrefetchScalarGridSpec(
                num_scalar_prefetch=1,
                grid=(count,),
                in_specs=[spec]
                + [whole((2 * M, depth_time))] * 2
                + [y_spec(), y_spec()]
                + [pl.BlockSpec(memory_space=pl.ANY)] * len(extra),
                out_specs=field_spec(),
            ),
            input_output_aliases={6: 0} if extra else {},
            compiler_params=params(),
            cost_estimate=pl.CostEstimate(
                flops=count * (6 * 2 * M * depth_time * cells + 6 * M * 2 * cells * width),
                bytes_accessed=count * (2 * cells * depth_time + 4 * M * width),
                transcendentals=0,
            ),
        )(order, values, t_high, t_low, y_high, y_low, *extra)

    grad_field = inverse(near, pair, None)
    grad_field = inverse(far, other, grad_field)
    return (grad_field, grad_weight)


def solution(mesh):
    in_specs = (
        P(None, "gx", "gy", None),
        P(None, "gx", "gy", None),
        P(None, "gx", None, None, "gy", None),
    )
    out_specs = (P(None, "gx", "gy", None), P(None, "gx", None, None, "gy", None))
    return jax.shard_map(
        per_device, mesh=mesh, in_specs=in_specs, out_specs=out_specs, check_vma=False
    )
```

```python
import functools
import math

import jax
import jax.numpy as jnp
import ml_dtypes
import numpy as np
from jax import lax
from jax.experimental import pallas as pl
from jax.experimental.pallas import tpu as pltpu
from jax.sharding import PartitionSpec as P

MX = 12
MY = 12
MZ = 12
MT = 8
Z = 64
T_SIZE = 16
KX = 24
KY = 24
M = 192
VMEM_LIMIT = 56 * 1024 * 1024

minor_contract = (((1,), (1,)), ((), ()))
plain_contract = (((1,), (0,)), ((), ()))
lead_contract = (((0,), (0,)), ((), ()))


def signed(count, half):
    ladder = np.arange(count)
    return np.where(ladder < half, ladder, ladder - 2 * half)


def split(table):
    table = np.asarray(table, np.float32)
    high = table.astype(ml_dtypes.bfloat16)
    low = (table - high.astype(np.float32)).astype(ml_dtypes.bfloat16)
    return high, low


def pair_table(count, half, length):
    residue = (signed(count, half)[:, None] * np.arange(length)[None, :]) % length
    phases = residue * (2.0 * math.pi / length)
    cosine = np.cos(phases) / math.sqrt(length)
    sine = np.sin(phases) / math.sqrt(length)
    return np.stack([np.stack([cosine, sine]), np.stack([-sine, cosine])])


def depth_table():
    cells = np.arange(Z * T_SIZE)
    modes = np.arange(M)
    depth_freq = signed(2 * MZ, MZ)[modes // MT]
    residue = (
        depth_freq[:, None] * (cells // T_SIZE)[None, :] * T_SIZE
        + (modes % MT)[:, None] * (cells % T_SIZE)[None, :] * Z
    ) % (Z * T_SIZE)
    phases = residue * (2.0 * math.pi / (Z * T_SIZE))
    scale = 1.0 / math.sqrt(Z * T_SIZE)
    return np.concatenate([np.cos(phases) * scale, -np.sin(phases) * scale])


def y_blocks(y_count, y_groups, x_local):
    table = pair_table(KY, MY, y_count).reshape(2, 2, KY, y_groups, -1)
    full = np.einsum("pqkgy,xw->gqxypwk", table, np.eye(x_local))
    return full.reshape(y_groups, 2 * x_local * table.shape[-1], 2 * x_local * KY)


def x_blocks(x_count, x_groups):
    table = pair_table(KX, MX, x_count).reshape(2, 2, KX, x_groups, -1)
    full = np.einsum("pqksx,yw->sqxykpw", table, np.eye(KY))
    return full.reshape(x_groups, 2 * table.shape[-1] * KY, KX * 2 * KY)


def halves(values):
    high = values.astype(jnp.bfloat16)
    return high, (values - high.astype(jnp.float32)).astype(jnp.bfloat16)


def mul(a, b, contract):
    return lax.dot_general(a, b, contract, preferred_element_type=jnp.float32)


def product(values, high, low, contract):
    v_high, v_low = halves(values)
    return (
        mul(v_high, low, contract) + mul(v_low, high, contract) + mul(v_high, high, contract)
    )


def params():
    return pltpu.CompilerParams(vmem_limit_bytes=VMEM_LIMIT)


def whole(shape):
    return pl.BlockSpec(shape, lambda *_: (0,) * len(shape))


def zt_y_kernel(rows_m, order, f_ref, g_ref, table, wh, wl, out):
    cells = jnp.concatenate(
        [ref[0].reshape(-1, ref.shape[-1]) for ref in (f_ref, g_ref)], axis=0
    )
    doubled = mul(table[...], cells, minor_contract)
    spectrum = doubled[: 2 * M] + doubled[2 * M :]
    half = spectrum.shape[1] // 2
    both = jnp.concatenate(
        [
            jnp.concatenate([spectrum[:M, at : at + half], spectrum[M:, at : at + half]], axis=1)
            for at in (0, half)
        ],
        axis=0,
    )
    planes = product(both, wh[0], wl[0], plain_contract)
    joined = jnp.concatenate([planes[:M], planes[M:]], axis=1)
    if rows_m % 8 == 0:
        out[0, :, 0] = joined.reshape(-1, rows_m, joined.shape[-1])
    else:
        out[0, 0] = joined


def x_kernel(last, r_ref, wh, wl, out, acc):
    step = pl.program_id(0)
    width = wh.shape[1]
    share = out.shape[2] // 2

    @pl.when(step == 0)
    def _():
        acc[...] = jnp.zeros_like(acc)

    for field in range(2):
        acc[field] += product(
            r_ref[0, :, field * width : (field + 1) * width], wh[0], wl[0], plain_contract
        )

    @pl.when(step == last)
    def _():
        for g in range(out.shape[0]):
            for field in range(2):
                out[g, :, field * share : (field + 1) * share] = acc[
                    field, :, g * share : (g + 1) * share
                ]


def back_kernel(v_ref, w_ref, s_ref, out, left, dual):
    share = v_ref.shape[2] // 2
    channels, kx_local = s_ref.shape[2:4]

    @pl.when(pl.program_id(0) == 0)
    def _():
        def one(o, carry):
            row = v_ref[o] * w_ref[...]
            row = jnp.concatenate([row, jnp.zeros((row.shape[0], 128), jnp.float32)], axis=1)
            for k in range(kx_local):
                at = 2 * k * KY
                real, imag = row[:, at : at + 128], row[:, at + KY : at + KY + 128]
                left[0, 0, o, k] = real
                left[0, 1, o, k] = -imag
                left[1, 0, o, k] = imag
                left[1, 1, o, k] = real
                at += share
                dual[0, o, k] = row[:, at : at + 128]
                dual[1, o, k] = row[:, at + KY : at + KY + 128]
            return carry

        lax.fori_loop(0, v_ref.shape[0], one, 0)

    for k in range(kx_local):
        real = jnp.zeros(s_ref.shape[4:], jnp.float32)
        imag = jnp.zeros(s_ref.shape[4:], jnp.float32)
        for o in range(channels):
            d_real, d_imag = dual[0, o, k, :, :KY], dual[1, o, k, :, :KY]
            s_real, s_imag = s_ref[0, 0, o, k], s_ref[1, 0, o, k]
            real += s_real * d_real + s_imag * d_imag
            imag += s_real * d_imag - s_imag * d_real
        at = 2 * k * KY
        out[0, :, at : at + KY] = real
        out[0, :, at + KY : at + 2 * KY] = imag


def x_back_kernel(b_ref, wh, wl, out, held):
    share = b_ref.shape[2]

    @pl.when(pl.program_id(0) == 0)
    def _():
        for g in range(b_ref.shape[0]):
            held[:, g * share : (g + 1) * share] = b_ref[g]

    out[0] = product(held[...], wh[0], wl[0], minor_contract)


def y_zt_back_kernel(order, q_ref, th, tl, wh, wl, *rest):
    out = rest[-1]
    rows = q_ref[...].reshape(M, q_ref.shape[-1])
    planes = product(rows, wh[0], wl[0], minor_contract)
    half = planes.shape[1] // 2
    stacked = jnp.concatenate([planes[:, :half], planes[:, half:]], axis=0)
    cells = product(stacked, th[...], tl[...], lead_contract)
    out[0] = cells.reshape(out.shape[1:]).astype(out.dtype)


def per_device(field_in, cotangent, spec_weight):
    channels, x_local, y_local, depth_time = field_in.shape
    n = lax.axis_size("gx")
    groups = lax.axis_size("gy")
    x_count, y_count = x_local * n, y_local * groups
    m_local = M // n
    kx_local = KX // groups
    c_local = channels // groups
    width = 2 * x_local * KY
    share = kx_local * 2 * KY
    cells = x_local * y_local
    aligned = m_local % 8 == 0
    me = lax.axis_index("gy")

    t_high, t_low = split(depth_table())
    t_both = np.concatenate([t_high, t_low])
    y_high, y_low = split(y_blocks(y_count, groups, x_local))
    x_high, x_low = split(x_blocks(x_count, n))

    ladder = lax.iota(jnp.int32, 2 * c_local)

    def order_of(first, second):
        owners = jnp.where(ladder < c_local, first, second)
        ids = owners * c_local + ladder % c_local
        return jnp.concatenate([ids, me[None]]).astype(jnp.int32)

    near = order_of(me, me ^ 2)
    far = order_of(me ^ 1, me ^ 3)
    count = 2 * c_local

    def field_spec():
        return pl.BlockSpec((1, x_local, y_local, depth_time), lambda i, o: (o[i], 0, 0, 0))

    def y_spec():
        return pl.BlockSpec((1, 2 * cells, width), lambda i, o: (o[count], 0, 0))

    if aligned:
        block = pl.BlockSpec(
            (1, n, 1, m_local, 2 * width), lambda i, o: (i // c_local, 0, i % c_local, 0, 0)
        )
        shape = (2, n, c_local, m_local, 2 * width)
    else:
        block = pl.BlockSpec(
            (1, 1, M, 2 * width), lambda i, o: (i // c_local, i % c_local, 0, 0)
        )
        shape = (2, c_local, M, 2 * width)

    def forward(order):
        result = pl.pallas_call(
            functools.partial(zt_y_kernel, m_local),
            out_shape=jax.ShapeDtypeStruct(shape, jnp.float32),
            grid_spec=pltpu.PrefetchScalarGridSpec(
                num_scalar_prefetch=1,
                grid=(count,),
                in_specs=[field_spec(), field_spec()]
                + [whole((4 * M, depth_time))]
                + [y_spec(), y_spec()],
                out_specs=block,
            ),
            compiler_params=params(),
            cost_estimate=pl.CostEstimate(
                flops=count * 2 * (4 * 2 * M * depth_time * cells + 6 * M * 2 * cells * width),
                bytes_accessed=count * (4 * cells * depth_time + 8 * M * width),
                transcendentals=0,
            ),
        )(order, field_in, cotangent, t_both, y_high, y_low)
        if not aligned:
            result = result.reshape(2, c_local, n, m_local, 2 * width).transpose(0, 2, 1, 3, 4)
        return result

    swap_core = [(d, d ^ 1) for d in range(groups)]
    swap_y = [(d, d ^ 2) for d in range(groups)]

    across = forward(order_of(me ^ 2, me ^ 3))
    for_y = across[0] + lax.ppermute(across[1], "gy", swap_core)
    for_y, here_order = lax.optimization_barrier((for_y, order_of(me, me ^ 1)))
    passed = lax.ppermute(for_y, "gy", swap_y)
    here = forward(here_order)
    summed = (here[0] + lax.ppermute(here[1], "gy", swap_core)) + passed

    section = lax.all_to_all(summed, "gx", split_axis=0, concat_axis=0, tiled=True)
    rows = c_local * m_local
    section = section.reshape(n, rows, 2 * width)
    x_spec = pl.BlockSpec((1, width, groups * share), lambda s: (s, 0, 0))
    at_kx = pl.pallas_call(
        functools.partial(x_kernel, n - 1),
        out_shape=jax.ShapeDtypeStruct((groups, rows, 2 * share), jnp.float32),
        grid=(n,),
        in_specs=[pl.BlockSpec((1, rows, 2 * width), lambda s: (s, 0, 0)), x_spec, x_spec],
        out_specs=whole((groups, rows, 2 * share)),
        scratch_shapes=[pltpu.VMEM((2, rows, groups * share), jnp.float32)],
        compiler_params=params(),
    )(section, x_high, x_low)
    modes = lax.all_to_all(at_kx, "gy", split_axis=0, concat_axis=0, tiled=True)
    modes = modes.reshape(channels, m_local, 2 * share)

    mode_ids = lax.axis_index("gx") * m_local + lax.iota(jnp.int32, m_local)
    doubling = jnp.where(mode_ids % MT == 0, 1.0, 2.0).astype(jnp.float32)
    lanes = lax.iota(jnp.int32, 2 * share)[None]
    doubling = jnp.where(lanes < share, 1.0, doubling[:, None])

    weights = jnp.transpose(spec_weight, (0, 2, 3, 4, 1, 5))
    unpacked = (channels, kx_local, m_local, 128)
    padded = 2 * channels * channels * kx_local * m_local * 128 * 4
    backward, left, dual = pl.pallas_call(
        back_kernel,
        out_shape=[
            jax.ShapeDtypeStruct((channels, m_local, share), jnp.float32),
            jax.ShapeDtypeStruct((2, 2) + unpacked, jnp.float32),
            jax.ShapeDtypeStruct((2,) + unpacked, jnp.float32),
        ],
        grid=(channels,),
        in_specs=[
            whole((channels, m_local, 2 * share)),
            whole((m_local, 2 * share)),
            pl.BlockSpec((2, 1, channels, kx_local, m_local, KY), lambda i: (0, i, 0, 0, 0, 0)),
        ],
        out_specs=[
            pl.BlockSpec((1, m_local, share), lambda i: (i, 0, 0)),
            whole((2, 2) + unpacked),
            whole((2,) + unpacked),
        ],
        compiler_params=params(),
        cost_estimate=pl.CostEstimate(flops=2 * padded, bytes_accessed=padded, transcendentals=0),
    )(modes, doubling, weights)

    spread = lax.all_to_all(
        backward.reshape(groups, rows, share), "gy", split_axis=0, concat_axis=0, tiled=True
    )
    left, dual = left[..., None, :, :, :KY], dual[:, None, None, ..., :KY]
    grad_weight = left[0] * dual[0] + left[1] * dual[1]
    grad_weight = jnp.transpose(grad_weight, (0, 4, 1, 2, 3, 5))

    planes = pl.pallas_call(
        x_back_kernel,
        out_shape=jax.ShapeDtypeStruct((n, rows, width), jnp.float32),
        grid=(n,),
        in_specs=[whole((groups, rows, share)), x_spec, x_spec],
        out_specs=pl.BlockSpec((1, rows, width), lambda s: (s, 0, 0)),
        scratch_shapes=[pltpu.VMEM((rows, groups * share), jnp.float32)],
        compiler_params=params(),
    )(spread, x_high, x_low)
    own = lax.all_to_all(planes, "gx", split_axis=0, concat_axis=0, tiled=True)
    own = own.reshape(n, c_local, m_local, width)
    crossed = lax.ppermute(own, "gy", swap_y)
    crossed, grad_weight = lax.optimization_barrier((crossed, grad_weight))
    pair = jnp.stack([own, crossed])
    other = lax.ppermute(pair, "gy", swap_core)

    def inverse(order, values, target):
        if aligned:
            spec = pl.BlockSpec(
                (1, n, 1, m_local, width), lambda i, o: (i // c_local, 0, i % c_local, 0, 0)
            )
        else:
            values = values.transpose(0, 2, 1, 3, 4).reshape(2, c_local, M, width)
            spec = pl.BlockSpec(
                (1, 1, M, width), lambda i, o: (i // c_local, i % c_local, 0, 0)
            )
        extra = [] if target is None else [target]
        return pl.pallas_call(
            y_zt_back_kernel,
            out_shape=jax.ShapeDtypeStruct(field_in.shape, jnp.bfloat16),
            grid_spec=pltpu.PrefetchScalarGridSpec(
                num_scalar_prefetch=1,
                grid=(count,),
                in_specs=[spec]
                + [whole((2 * M, depth_time))] * 2
                + [y_spec(), y_spec()]
                + [pl.BlockSpec(memory_space=pl.ANY)] * len(extra),
                out_specs=field_spec(),
            ),
            input_output_aliases={6: 0} if extra else {},
            compiler_params=params(),
            cost_estimate=pl.CostEstimate(
                flops=count * (6 * 2 * M * depth_time * cells + 6 * M * 2 * cells * width),
                bytes_accessed=count * (2 * cells * depth_time + 4 * M * width),
                transcendentals=0,
            ),
        )(order, values, t_high, t_low, y_high, y_low, *extra)

    grad_field = inverse(near, pair, None)
    grad_field = inverse(far, other, grad_field)
    return (grad_field, grad_weight)


def solution(mesh):
    in_specs = (
        P(None, "gx", "gy", None),
        P(None, "gx", "gy", None),
        P(None, "gx", None, None, "gy", None),
    )
    out_specs = (P(None, "gx", "gy", None), P(None, "gx", None, None, "gy", None))
    return jax.shard_map(
        per_device, mesh=mesh, in_specs=in_specs, out_specs=out_specs, check_vma=False
    )
```
